256 devices in a mesh: grp: 16 (over y_hi, z), blk: 16 (over x, y_lo, core).
Axes of the slice: x: 4, y: 4 (y_hi: 2, y_lo: 2; y = y_hi * 2 + y_lo), z: 8, core: 2. Of those that a mesh axis runs over, the one named last changes fastest.
Arguments:
- points: float32 [65536, 64], P(('blk', 'grp')), may hold values from -4.6 to 4.6
- lengthscale: float32 [64], replicated, may hold values from 2.56 to 10.16
- noise: float32 [65536], P(('blk', 'grp')), may hold values from 0.01 to 1
- solution: float32 [65536, 32], P(('blk', 'grp')), may hold values from -6 to 6
- residual: float32 [65536, 32], P(('blk', 'grp')), may hold values from -1.2 to 1.2
- direction: float32 [65536, 32], P(('blk', 'grp')), may hold values from -6 to 6
Outputs:
- new_solution: float32 [65536, 32], P(('blk', 'grp'))
- new_residual: float32 [65536, 32], P(('blk', 'grp'))
- new_direction: float32 [65536, 32], P(('blk', 'grp'))
The draws below stay inside these ranges and needn't reach their ends.
All inputs are finite; a program needn't handle non-finite values.
Results may differ from the reference program's by a relative error of at most 0.009.
Values may be sent and summed in bfloat16 or wider, within the bound.
A program may use at most 64 MiB of HBM per device.

```python
import math
import jax
import jax.numpy as jnp
from jax import lax

DIM = 64
RHS = 32
ROWS = 65536


def draw_points(key, part):
    key = jax.random.fold_in(key, 3)
    member_key, center_key, offset_key = jax.random.split(key, 3)
    clusters = ROWS // 32
    member = jax.random.randint(member_key, (ROWS,), 0, clusters)
    centers = 1.29 * jax.random.truncated_normal(center_key, -2.6, 2.6, (clusters, DIM), jnp.float32)
    offsets = 0.434 * jax.random.truncated_normal(offset_key, -2.6, 2.6, (ROWS, DIM), jnp.float32)
    return centers[member] + offsets


def draw_residual(key, part):
    key = jax.random.fold_in(key, 7)
    ramp = 0.1 + 0.2 * jnp.arange(ROWS, dtype=jnp.float32) / ROWS
    values = jax.random.truncated_normal(key, -4.0, 4.0, (ROWS, RHS), jnp.float32)
    return values * ramp[:, None]


def block_scale(stream_key, shape, cuts, smallest, largest):
    factor_of = 1.0
    for axis_at, blocks in cuts:
        heights = jax.random.uniform(jax.random.fold_in(jax.random.fold_in(stream_key, 6), axis_at), (blocks,), jnp.float32, smallest / len(cuts), largest / len(cuts))
        factor_of = factor_of * jnp.repeat(jnp.exp(heights), shape[axis_at] // blocks).reshape((-1,) + (1,) * (len(shape) - 1 - axis_at))
    return factor_of


def centred(stream_key, extent, width, bound, pieces=(), held_as=jnp.bfloat16):
    drawn = jax.random.normal(stream_key, extent, jnp.float32) * width
    if len(pieces) > 0:
        drawn = block_scale(stream_key, extent, pieces, -0.22, 0.18) * drawn
    return jnp.clip(drawn, min=-bound, max=bound).astype(held_as)


def setup_inputs(seed: int = 0) -> dict:
    key_list = jax.random.split(jax.random.key(seed), 7)
    points = draw_points(jax.random.fold_in(key_list[6], 71), 0)
    lengthscale = jnp.clip(jnp.exp(jax.random.uniform(key_list[1], (DIM,), jnp.float32, math.log(2.56), math.log(10.16))), 2.56, 10.16)
    noise = jnp.clip(jnp.exp(math.log(1.0) - 4.6051702 * jax.random.uniform(key_list[2], (ROWS,), jnp.float32) ** block_scale(key_list[2], (ROWS,), ((0, 256),), -0.2, 0.2)), 0.01, 1.0)
    solution = centred(key_list[3], (ROWS, RHS), 1.0, 6.0, ((0, 256),), jnp.float32)
    residual = draw_residual(jax.random.fold_in(key_list[6], 71), 0)
    direction = centred(key_list[5], (ROWS, RHS), 1.0, 6.0, ((0, 256),), jnp.float32)
    return {"points": points, "lengthscale": lengthscale, "noise": noise, "solution": solution, "residual": residual, "direction": direction}


def kernel_block(rows, rows_sq, cols, cols_sq):
    cross = jnp.einsum('id,jd->ij', rows.astype(jnp.float32), cols.astype(jnp.float32))
    dist_sq = rows_sq[:, None] + cols_sq[None, :] - 2.0 * cross
    radius = jnp.sqrt(jnp.maximum(dist_sq, 1e-06))
    shaped = jnp.sqrt(5.0) * radius
    return ((1.0 + shaped + shaped * shaped / 3.0) * jnp.exp(-shaped)).astype(jnp.bfloat16)

def reference(points, lengthscale, noise, solution, residual, direction):
    scaled = (points / lengthscale[None, :]).astype(jnp.bfloat16)
    sq_all = lax.optimization_barrier(jnp.sum(jnp.square(scaled.astype(jnp.float32)), axis=1))
    dir_b = direction.astype(jnp.bfloat16)
    block = 256
    count = ROWS // block
    row_sets = scaled.reshape(count, block, DIM)
    sq_sets = sq_all.reshape(count, block)

    def one_block(pair):
        rows, rows_sq = pair
        kern = kernel_block(rows, rows_sq, scaled, sq_all)
        return jnp.dot(kern, dir_b, preferred_element_type=jnp.float32)
    product = lax.map(one_block, (row_sets, sq_sets)).reshape(ROWS, RHS)
    image = product + noise[:, None] * direction
    rr = lax.optimization_barrier(jnp.sum(residual * residual, axis=0))
    curv = lax.optimization_barrier(jnp.sum(direction * image, axis=0))
    alpha = rr / curv
    new_solution = solution + alpha[None, :] * direction
    new_residual = residual - alpha[None, :] * image
    new_rr = lax.optimization_barrier(jnp.sum(new_residual * new_residual, axis=0))
    new_direction = new_residual + (new_rr / rr)[None, :] * direction
    return (new_solution, new_residual, new_direction)
```

```python
import functools

import jax
import jax.numpy as jnp
from jax import lax
from jax.experimental import pallas as pl
from jax.experimental.pallas import tpu as pltpu
from jax.sharding import PartitionSpec as P

MESH = pl.DeviceIdType.MESH
F32 = jnp.float32
BF16 = jnp.bfloat16
NT = (((1,), (1,)), ((), ()))

DIM = 64
RHS = 32
BLK = 256
AUG = 16
FEAT = DIM + AUG
PAY = FEAT + RHS
SIDE = 16
PANEL1 = (0, 1, -2, -3)
PANEL2 = (8, -4, -5, 6, 7)
ROWS = PANEL1 + PANEL2
EXPO = -3.2259641843312467
LIN = 1.3416407864998738


def matern(d2):
    d2 = jnp.maximum(d2, 1e-6)
    r = d2 * lax.rsqrt(d2)
    return ((r * (r + LIN) + 0.6) * jnp.exp2(r * EXPO)).astype(BF16)


def place():
    g, b = lax.axis_index("grp"), lax.axis_index("blk")
    p = (g % 8) * 2 + b % 2
    q = (b // 4) * 4 + (g // 8) * 2 + (b // 2) % 2
    return p, q


def device(p, q):
    p, q = lax.rem(p + 32, SIDE), lax.rem(q + 32, SIDE)
    x, y = q // 4, q % 4
    return {"grp": (y // 2) * 8 + p // 2, "blk": x * 4 + (y % 2) * 2 + p % 2}


def kernel(pts, scale, noise, sol, res, direc, out_sol, out_res, out_dir,
           cols, rowpay, rowland, amat, dmat1, dmat2, acc_i, acc_j, ks, ks2, ret, stat, stat2, land1, land2,
           col_sem, row_sem, pay_sem, ret_sem, back_sem, s1_sem, s2_sem, st_sem):
    p, q = place()
    barrier = pltpu.get_barrier_semaphore()

    def greet(k, c):
        pl.semaphore_signal(barrier, inc=1, device_id=device(p + k, q), device_id_type=MESH)
        pl.semaphore_signal(barrier, inc=1, device_id=device(p, q + k), device_id_type=MESH)
        return c

    lax.fori_loop(1, SIDE, greet, 0)

    scaled = (pts[...] / scale[...]).astype(BF16)
    wide = scaled.astype(F32)
    sq = jnp.sum(wide * wide, axis=0, keepdims=True)
    hi = sq.astype(BF16).astype(F32)
    mid = (sq - hi).astype(BF16).astype(F32)
    low = sq - hi - mid
    at = lax.broadcasted_iota(jnp.int32, (AUG, BLK), 0)

    def aug(ones, parts):
        out = jnp.where((at >= ones) & (at < ones + 3), 1.0, 0.0)
        for n, part in enumerate((hi, mid, low)):
            out = jnp.where(at == parts + n, part, out)
        return out.astype(BF16)

    dir_b = direc[...].astype(BF16)
    cols[0, 0:DIM, :] = scaled
    cols[0, DIM:FEAT, :] = aug(0, 3)
    cols[0, FEAT:PAY, :] = dir_b
    rowpay[0:DIM, :] = (wide * -2.0).astype(BF16)
    rowpay[DIM:FEAT, :] = aug(3, 0)
    rowpay[FEAT:PAY, :] = dir_b
    for k in range(SIDE):
        cols[k, PAY:, :] = jnp.zeros((128 - PAY, BLK), BF16)
    acc_i[...] = jnp.zeros_like(acc_i)
    acc_j[...] = jnp.zeros_like(acc_j)

    pl.semaphore_wait(barrier, 2 * (SIDE - 1))

    def send_row(k):
        return pltpu.make_async_remote_copy(
            src_ref=rowpay, dst_ref=rowland.at[k], send_sem=pay_sem, recv_sem=row_sem.at[k],
            device_id=device(p - ROWS[k], q), device_id_type=MESH)

    def send_col(k):
        return pltpu.make_async_remote_copy(
            src_ref=cols.at[0, pl.ds(0, PAY)], dst_ref=cols.at[k, pl.ds(0, PAY)], send_sem=pay_sem,
            recv_sem=col_sem.at[k], device_id=device(p, q - k), device_id_type=MESH)

    def back_row(k):
        return pltpu.make_async_remote_copy(
            src_ref=acc_i.at[k], dst_ref=ret.at[k - 1], send_sem=back_sem, recv_sem=ret_sem,
            device_id=device(p + ROWS[k], q), device_id_type=MESH)

    def back_col(k):
        return pltpu.make_async_remote_copy(
            src_ref=acc_j.at[k], dst_ref=ret.at[k + 7], send_sem=back_sem, recv_sem=ret_sem,
            device_id=device(p, q + k), device_id_type=MESH)

    for k in range(1, 4):
        send_row(k).start()

    def start_col(k, c):
        send_col(k).start()
        return c

    lax.fori_loop(1, SIDE, start_col, 0)
    for k in range(4, 9):
        send_row(k).start()

    def take_row(k, block):
        dmat, first = (dmat1, 0) if k < 4 else (dmat2, 4)
        wide = jnp.concatenate([block[0:FEAT, :], jnp.zeros((128 - FEAT, BLK), BF16)], axis=0)
        amat[k * BLK:(k + 1) * BLK, :] = wide.T
        at = slice((k - first) * BLK, (k - first + 1) * BLK)
        d = block[FEAT:PAY, :]
        dmat[0, :, at] = d
        dmat[1, :, at] = jnp.zeros_like(d) if k == first else d

    take_row(0, rowpay)
    for k in range(1, 4):
        send_row(k).wait_recv()
        take_row(k, rowland.at[k])

    def tile(rows, c):
        a = amat[rows[0] * BLK:(rows[1]) * BLK, :]
        return matern(jnp.dot(a, cols[c], preferred_element_type=F32))

    def give(rows, c, kern):
        c = jnp.int32(c)
        dmat, first = (dmat1, 0) if rows[1] <= 4 else (dmat2, 4)
        half = jnp.where(lax.rem(c, 8) == 0, 1, 0) if rows[0] == first else 0
        d = dmat[half, :, (rows[0] - first) * BLK:(rows[1] - first) * BLK]
        acc_j[c] += jnp.dot(d, kern, preferred_element_type=F32)
        part = lax.dot_general(cols[c, FEAT:PAY, :], kern, NT, preferred_element_type=F32)
        for n, k in enumerate(range(*rows)):
            acc_i[k] += part[:, n * BLK:(n + 1) * BLK]

    def height(rows):
        return (rows[1] - rows[0]) * BLK

    def phase(full, most, waits, backs, before):
        hf, hm = height(full), height(most)
        new = tile(full, 0)
        if before is not None:
            give(*before)
        ks[0:hf, :] = new

        def step(c, rows_new, rows_old, src, dst):
            new = tile(rows_new, c)
            give(rows_old, c - 1, src[0:height(rows_old), :])
            dst[0:height(rows_new), :] = new

        def pair(rows):
            def body(n, carry):
                c = carry
                if waits:
                    send_col(c).wait_recv()
                    send_col(c + 1).wait_recv()
                step(c, rows, rows, *((ks, ks2) if rows == full else (ks2, ks)))
                step(c + 1, rows, rows, *((ks2, ks) if rows == full else (ks, ks2)))
                if backs:
                    @pl.when(c > 1)
                    def _():
                        back_col(c - 1).start()
                    back_col(c).start()
                return c + 2
            return body

        lax.fori_loop(0, 4, pair(full), 1)
        if waits:
            send_col(9).wait_recv()
        step(9, most, full, ks, ks2)
        if backs:
            back_col(8).start()
        lax.fori_loop(0, 3, pair(most), 10)

    phase((0, 4), (1, 4), True, False, None)
    for k in range(4, 9):
        send_row(k).wait_recv()
        take_row(k, rowland.at[k])
    phase((4, 9), (5, 9), False, True, ((1, 4), 15, ks2[0:3 * BLK, :]))
    give((5, 9), 15, ks2[0:4 * BLK, :])
    back_col(15).start()
    for k in range(1, 9):
        back_row(k).start()

    pltpu.make_async_remote_copy(src_ref=ret, dst_ref=ret, send_sem=back_sem, recv_sem=ret_sem,
                                 device_id=device(p + 1, q), device_id_type=MESH).wait_recv()
    total = acc_i[0] + acc_j[0]
    for k in range(23):
        total += ret[k]
    d, r = direc[...], res[...]
    image = total * (5.0 / 3.0) + noise[...] * d
    lane = lax.broadcasted_iota(jnp.int32, (RHS, 128), 1)

    def put(n, v):
        return jnp.where(lane == n, jnp.sum(v, axis=1, keepdims=True), 0.0)

    stat[...] = put(0, r * r) + put(1, d * image) + put(2, r * image) + put(3, image * image)

    def share(src, land, sem, along_p):
        def copy(k):
            to = device(p - k, q) if along_p else device(p, q - k)
            return pltpu.make_async_remote_copy(src_ref=src, dst_ref=land.at[k - 1], send_sem=st_sem,
                                                recv_sem=sem, device_id=to, device_id_type=MESH)

        def start(k, c):
            copy(k).start()
            return c

        lax.fori_loop(1, SIDE, start, 0)
        pltpu.make_async_remote_copy(src_ref=land, dst_ref=land, send_sem=st_sem, recv_sem=sem,
                                     device_id=device(p + 1, q), device_id_type=MESH).wait_recv()
        out = src[...]
        for k in range(SIDE - 1):
            out += land[k]
        return out

    stat2[...] = share(stat, land1, s1_sem, True)
    sums = share(stat2, land2, s2_sem, False)
    rr, curv, rq, qq = (sums[:, n:n + 1] for n in range(4))
    alpha = rr / curv
    new_rr = rr - alpha * (2.0 * rq - alpha * qq)
    beta = new_rr / rr
    out_sol[...] = sol[...] + alpha * d
    new_res = r - alpha * image
    out_res[...] = new_res
    out_dir[...] = new_res + beta * d

    def sent(ref, sem):
        pltpu.make_async_remote_copy(src_ref=ref, dst_ref=ref, send_sem=sem, recv_sem=ret_sem,
                                     device_id=device(p + 1, q), device_id_type=MESH).wait_send()

    sent(rowland.at[pl.ds(1, 8)], pay_sem)
    for k in range(1, SIDE):
        sent(cols.at[k, pl.ds(0, PAY)], pay_sem)
    sent(ret, back_sem)
    sent(land1, st_sem)
    sent(land2, st_sem)


def local(points, lengthscale, noise, solution, residual, direction):
    vmem = pl.BlockSpec(memory_space=pltpu.VMEM)
    out = jax.ShapeDtypeStruct((RHS, BLK), F32)
    dma = pltpu.SemaphoreType.DMA
    new_sol, new_res, new_dir = pl.pallas_call(
        kernel,
        out_shape=(out, out, out),
        in_specs=[vmem] * 6,
        out_specs=(vmem,) * 3,
        scratch_shapes=[
            pltpu.VMEM((SIDE, 128, BLK), BF16),
            pltpu.VMEM((PAY, BLK), BF16),
            pltpu.VMEM((9, PAY, BLK), BF16),
            pltpu.VMEM((9 * BLK, 128), BF16),
            pltpu.VMEM((2, RHS, 4 * BLK), BF16),
            pltpu.VMEM((2, RHS, 5 * BLK), BF16),
            pltpu.VMEM((9, RHS, BLK), F32),
            pltpu.VMEM((SIDE, RHS, BLK), F32),
            pltpu.VMEM((5 * BLK, BLK), BF16),
            pltpu.VMEM((5 * BLK, BLK), BF16),
            pltpu.VMEM((23, RHS, BLK), F32),
            pltpu.VMEM((RHS, 128), F32),
            pltpu.VMEM((RHS, 128), F32),
            pltpu.VMEM((SIDE - 1, RHS, 128), F32),
            pltpu.VMEM((SIDE - 1, RHS, 128), F32),
            dma((SIDE,)),
            dma((9,)),
            dma,
            dma,
            dma,
            dma,
            dma,
            dma,
        ],
        compiler_params=pltpu.CompilerParams(
            collective_id=0, has_side_effects=True, vmem_limit_bytes=40 * 2**20),
        name="cg_step",
    )(points.T, lengthscale[:, None], noise[None, :], solution.T, residual.T, direction.T)
    return new_sol.T, new_res.T, new_dir.T


def solution(mesh):
    rows = P(("blk", "grp"), None)
    in_specs = (rows, P(), P(("blk", "grp")), rows, rows, rows)
    return jax.shard_map(local, mesh=mesh, in_specs=in_specs, out_specs=(rows,) * 3, check_vma=False)
```

```python
import jax
import jax.numpy as jnp
from jax import lax
from jax.experimental import pallas as pl
from jax.experimental.pallas import tpu as pltpu
from jax.sharding import PartitionSpec as P

MESH = pl.DeviceIdType.MESH
F32 = jnp.float32
BF16 = jnp.bfloat16
NT = (((1,), (1,)), ((), ()))

DIM = 64
RHS = 32
BLK = 256
AUG = 16
FEAT = DIM + AUG
PAY = FEAT + RHS
SIDE = 16
PANEL1 = (0, 1, -4, 3)
PANEL2 = (8, -5, 2, 6, -7)
ROWS = PANEL1 + PANEL2
F1, M1 = (0, 4), (1, 4)
F2, M2 = (4, 9), (5, 9)
EXPO = -3.2259641843312467
LIN = 1.3416407864998738


def matern(d2):
    d2 = jnp.maximum(d2, 1e-6)
    r = d2 * lax.rsqrt(d2)
    return ((r * (r + LIN) + 0.6) * jnp.exp2(r * EXPO)).astype(BF16)


def place():
    g, b = lax.axis_index("grp"), lax.axis_index("blk")
    return (b // 4) * 4 + (g // 8) * 2 + (b // 2) % 2, (g % 8) * 2 + b % 2


def device(p, q):
    p, q = lax.rem(p + 32, SIDE), lax.rem(q + 32, SIDE)
    x, y = p // 4, p % 4
    return {"grp": (y // 2) * 8 + q // 2, "blk": x * 4 + (y % 2) * 2 + q % 2}


def slot(k):
    return lax.rem(k + 32, SIDE)


def kernel(pts_hbm, scale_hbm, noise_hbm, res_hbm, dir_hbm, image_out, alpha_out, beta_out,
           pts, scale, noise, res, direc,
           cols, rowpay, rowland, amat, dmat, acc_i, acc_j, back_i, back_j, ks, ks2, ret, stat, stat2, land1, land2,
           in_sem, col_sem, row_sem, pay_sem, fwd_sem, ret_sem, back_sem, s1_sem, s2_sem, st_sem):
    p, q = place()
    turn = 1 - 2 * lax.rem(q, 2)
    barrier = pltpu.get_barrier_semaphore()

    def greet(k, c):
        pl.semaphore_signal(barrier, inc=1, device_id=device(p + k, q), device_id_type=MESH)
        pl.semaphore_signal(barrier, inc=1, device_id=device(p, q + k), device_id_type=MESH)
        return c

    lax.fori_loop(1, SIDE, greet, 0)
    fetch = [pltpu.make_async_copy(a, b, in_sem.at[n]) for n, (a, b) in enumerate(
        ((pts_hbm, pts), (scale_hbm, scale), (dir_hbm, direc), (res_hbm, res), (noise_hbm, noise)))]
    for f in fetch:
        f.start()
    for k in range(SIDE):
        cols[k, PAY:, :] = jnp.zeros((128 - PAY, BLK), BF16)
    acc_i[...] = jnp.zeros_like(acc_i)
    for f in fetch[:3]:
        f.wait()

    at = lax.broadcasted_iota(jnp.int32, (DIM, DIM), 0) == lax.broadcasted_iota(jnp.int32, (DIM, DIM), 1)
    scale_col = jnp.sum(jnp.where(at, scale[...], 0.0), axis=1, keepdims=True)
    scaled = (pts[...] / scale_col).astype(BF16)
    wide = scaled.astype(F32)
    sq = jnp.sum(wide * wide, axis=0, keepdims=True)
    hi = sq.astype(BF16).astype(F32)
    mid = (sq - hi).astype(BF16).astype(F32)
    low = sq - hi - mid
    row = lax.broadcasted_iota(jnp.int32, (AUG, BLK), 0)

    def aug(ones, parts):
        out = jnp.where((row >= ones) & (row < ones + 3), 1.0, 0.0)
        for n, part in enumerate((hi, mid, low)):
            out = jnp.where(row == parts + n, part, out)
        return out.astype(BF16)

    dir_b = direc[...].astype(BF16)
    cols[0, 0:DIM, :] = scaled
    cols[0, DIM:FEAT, :] = aug(0, 3)
    cols[0, FEAT:PAY, :] = dir_b
    rowpay[0:DIM, :] = (wide * -2.0).astype(BF16)
    rowpay[DIM:FEAT, :] = aug(3, 0)
    rowpay[FEAT:PAY, :] = dir_b

    pl.semaphore_wait(barrier, 2 * (SIDE - 1))

    def send_row(k):
        return pltpu.make_async_remote_copy(
            src_ref=rowpay, dst_ref=rowland.at[k], send_sem=pay_sem, recv_sem=row_sem.at[k],
            device_id=device(p - ROWS[k], q), device_id_type=MESH)

    def send_col(k, to=None, sem=None):
        k, to = slot(k), slot(k if to is None else to)
        return pltpu.make_async_remote_copy(
            src_ref=cols.at[k, pl.ds(0, PAY)], dst_ref=cols.at[to, pl.ds(0, PAY)],
            send_sem=pay_sem if sem is None else sem,
            recv_sem=col_sem.at[to], device_id=device(p, q + k - to), device_id_type=MESH)

    def arrived(k):
        send_col(k, k).wait_recv()

    def share_core(k):
        send_col(k, k - turn, fwd_sem).start()

    for k in range(1, 4):
        send_row(k).start()
    send_col(0, 2).start()
    send_col(0, -2).start()
    share_core(0)
    send_col(0, 4).start()
    send_col(0, -4).start()

    def take_row(k, block):
        wide = jnp.concatenate([block[0:FEAT, :], jnp.zeros((128 - FEAT, BLK), BF16)], axis=0)
        amat[k * BLK:(k + 1) * BLK, :] = wide.T
        dmat[:, k * BLK:(k + 1) * BLK] = block[FEAT:PAY, :]

    take_row(0, rowpay)
    for k in range(4, 9):
        send_row(k).start()
    for k in range(1, 4):
        send_row(k).wait_recv()
        take_row(k, rowland.at[k])

    def tile(rows, c):
        a = amat[rows[0] * BLK:rows[1] * BLK, :]
        return matern(jnp.dot(a, cols[slot(c)], preferred_element_type=F32))

    def height(rows):
        return (rows[1] - rows[0]) * BLK

    def give(rows, c, kern, twice=False):
        first = rows[0] + 1 if twice else rows[0]
        skip = (first - rows[0]) * BLK
        k = slot(c)
        part = jnp.dot(dmat[:, first * BLK:rows[1] * BLK], kern[skip:, :], preferred_element_type=F32)
        if rows[1] <= 4:
            acc_j[k] = part
        elif isinstance(c, int) and c == 0:
            acc_j[k] += part
        else:
            back_j[k] = (acc_j[k] + part).astype(BF16)
        part = lax.dot_general(cols[k, FEAT:PAY, :], kern, NT, preferred_element_type=F32)
        for n, r in enumerate(range(*rows)):
            acc_i[r] += part[:, n * BLK:(n + 1) * BLK]

    def step(rows, c, old, c_old, src, dst, twice=False):
        new = tile(rows, c)
        give(old, c_old, src[0:height(old), :], twice)
        dst[0:height(rows), :] = new

    def back_row(k):
        return pltpu.make_async_remote_copy(
            src_ref=back_i.at[k - 1], dst_ref=ret.at[k - 1], send_sem=back_sem, recv_sem=ret_sem,
            device_id=device(p + ROWS[k], q), device_id_type=MESH)

    def back_col(k):
        k = slot(k)
        return pltpu.make_async_remote_copy(
            src_ref=back_j.at[k], dst_ref=ret.at[k + 7], send_sem=back_sem, recv_sem=ret_sem,
            device_id=device(p, q + k), device_id_type=MESH)

    ks[0:height(F1), :] = tile(F1, 0)
    for k in (2, -2):
        arrived(k)
        share_core(k)
    arrived(1)
    arrived(-1)
    step(F1, 1, F1, 0, ks, ks2, twice=True)

    def near(m, carry):
        @pl.when(m == 2)
        def _():
            for k in (4, -4):
                arrived(k)
                share_core(k)
            send_col(4, 6).start()
            send_col(-4, -6).start()
            send_col(4, 8).start()
            arrived(3)
            arrived(-3)

        step(M1, -m, F1, m, ks2, ks)
        step(F1, m + 1, M1, -m, ks, ks2)
        return carry

    lax.fori_loop(1, 4, near, 0)
    step(M1, -4, F1, 4, ks2, ks)

    for k in range(4, 9):
        send_row(k).wait_recv()
        take_row(k, rowland.at[k])
    step(F2, 4, M1, -4, ks, ks2)

    def home_near(n, carry):
        m = 4 - n
        step(M2, -m, F2, m, ks2, ks)
        back_col(m).start()
        step(F2, m - 1, M2, -m, ks, ks2)
        back_col(-m).start()
        return carry

    lax.fori_loop(0, 2, home_near, 0)
    for k in (6, -6, 8):
        arrived(k)
        share_core(k)
    step(M2, -2, F2, 2, ks2, ks)
    back_col(2).start()

    for k in (5, -5, 7, -7):
        arrived(k)
    step(F1, 5, M2, -2, ks, ks2)
    back_col(-2).start()

    def far(m, carry):
        step(M1, -m, F1, m, ks2, ks)
        step(F1, m + 1, M1, -m, ks, ks2)
        return carry

    lax.fori_loop(5, 8, far, 0)

    step(F2, 8, F1, 8, ks2, ks, twice=True)
    for k in range(1, 4):
        back_i[k - 1] = acc_i[k].astype(BF16)
        back_row(k).start()
    step(F2, 7, F2, 8, ks, ks2, twice=True)
    back_col(8).start()

    def home(n, carry):
        m = jnp.where(n < 3, 7 - n, 1)
        step(M2, -m, F2, m, ks2, ks)
        back_col(m).start()
        step(F2, jnp.where(n < 2, 6 - n, 3 - n), M2, -m, ks, ks2)
        back_col(-m).start()
        return carry

    lax.fori_loop(0, 4, home, 0)
    give(F2, 0, ks2[0:height(F2), :], twice=True)
    for k in range(4, 9):
        back_i[k - 1] = acc_i[k].astype(BF16)
        back_row(k).start()

    total = acc_i[0] + acc_j[0]
    for f in fetch[3:]:
        f.wait()
    pltpu.make_async_remote_copy(src_ref=ret, dst_ref=ret, send_sem=back_sem, recv_sem=ret_sem,
                                 device_id=device(p + 1, q), device_id_type=MESH).wait_recv()
    for k in range(23):
        total += ret[k].astype(F32)
    d, r = direc[...], res[...]
    image = total * (5.0 / 3.0) + noise[...] * d
    image_out[...] = image
    lane = lax.broadcasted_iota(jnp.int32, (RHS, 128), 1)
    rhs = lax.broadcasted_iota(jnp.int32, (RHS, 128), 0)

    packed = jnp.zeros((RHS, 128), F32)
    for n, v in enumerate((r * r, d * image, r * image, image * image)):
        packed = jnp.where(lane == rhs + n * RHS, jnp.sum(v, axis=1, keepdims=True), packed)
    stat[...] = jnp.sum(packed, axis=0, keepdims=True)

    def share(src, land, sem, along_p):
        def copy(k):
            to = device(p - k, q) if along_p else device(p, q - k)
            return pltpu.make_async_remote_copy(src_ref=src, dst_ref=land.at[k - 1], send_sem=st_sem,
                                                recv_sem=sem, device_id=to, device_id_type=MESH)

        def start(n, c):
            copy(8 + ((n + 1) // 2) * (1 - 2 * lax.rem(n, 2))).start()
            return c

        lax.fori_loop(0, SIDE - 1, start, 0)
        pltpu.make_async_remote_copy(src_ref=land, dst_ref=land, send_sem=st_sem, recv_sem=sem,
                                     device_id=device(p + 1, q), device_id_type=MESH).wait_recv()
        out = src[...]
        for k in range(SIDE - 1):
            out += land[k]
        return out

    stat2[...] = share(stat, land1, s1_sem, False)
    sums = share(stat2, land2, s2_sem, True)
    rr, curv, rq, qq = (jnp.sum(jnp.where(lane == rhs + n * RHS, sums, 0.0), axis=1, keepdims=True)
                        for n in range(4))
    alpha = rr / curv
    new_rr = rr - alpha * (2.0 * rq - alpha * qq)
    alpha_out[...] = jnp.broadcast_to(alpha, (RHS, BLK))
    beta_out[...] = jnp.broadcast_to(new_rr / rr, (RHS, BLK))

    def sent(ref, sem):
        pltpu.make_async_remote_copy(src_ref=ref, dst_ref=ref, send_sem=sem, recv_sem=ret_sem,
                                     device_id=device(p + 1, q), device_id_type=MESH).wait_send()

    sent(rowland.at[pl.ds(1, 8)], pay_sem)
    for k in range(7):
        sent(rowpay, pay_sem)
    sent(rowland.at[pl.ds(1, 8)], fwd_sem)
    sent(ret, back_sem)
    sent(land1, st_sem)
    sent(land2, st_sem)


def local(points, lengthscale, noise, solution, residual, direction):
    vmem = pl.BlockSpec(memory_space=pltpu.VMEM)
    out = jax.ShapeDtypeStruct((RHS, BLK), F32)
    dma = pltpu.SemaphoreType.DMA
    res_t, dir_t = residual.T, direction.T
    image, alpha, beta = pl.pallas_call(
        kernel,
        out_shape=(out, out, out),
        in_specs=[pl.BlockSpec(memory_space=pltpu.HBM)] * 5,
        out_specs=(vmem,) * 3,
        scratch_shapes=[
            pltpu.VMEM((DIM, BLK), F32),
            pltpu.VMEM((1, DIM), F32),
            pltpu.VMEM((1, BLK), F32),
            pltpu.VMEM((RHS, BLK), F32),
            pltpu.VMEM((RHS, BLK), F32),
            pltpu.VMEM((SIDE, 128, BLK), BF16),
            pltpu.VMEM((PAY, BLK), BF16),
            pltpu.VMEM((9, PAY, BLK), BF16),
            pltpu.VMEM((9 * BLK, 128), BF16),
            pltpu.VMEM((RHS, 9 * BLK), BF16),
            pltpu.VMEM((9, RHS, BLK), F32),
            pltpu.VMEM((SIDE, RHS, BLK), F32),
            pltpu.VMEM((8, RHS, BLK), BF16),
            pltpu.VMEM((SIDE, RHS, BLK), BF16),
            pltpu.VMEM((5 * BLK, BLK), BF16),
            pltpu.VMEM((5 * BLK, BLK), BF16),
            pltpu.VMEM((23, RHS, BLK), BF16),
            pltpu.VMEM((1, 128), F32),
            pltpu.VMEM((1, 128), F32),
            pltpu.VMEM((SIDE - 1, 1, 128), F32),
            pltpu.VMEM((SIDE - 1, 1, 128), F32),
            dma((5,)),
            dma((SIDE,)),
            dma((9,)),
        ] + [dma] * 7,
        compiler_params=pltpu.CompilerParams(
            collective_id=0, has_side_effects=True, vmem_limit_bytes=63 * 2**20),
        name="cg_step",
    )(points.T, lengthscale[None, :], noise[None, :], res_t, dir_t)
    new_sol = solution.T + alpha * dir_t
    new_res = res_t - alpha * image
    new_dir = new_res + beta * dir_t
    return new_sol.T, new_res.T, new_dir.T


def solution(mesh):
    rows = P(("blk", "grp"), None)
    in_specs = (rows, P(), P(("blk", "grp")), rows, rows, rows)
    return jax.shard_map(local, mesh=mesh, in_specs=in_specs, out_specs=(rows,) * 3, check_vma=False)
```

```python
import jax
import jax.numpy as jnp
from jax import lax
from jax.experimental import pallas as pl
from jax.experimental.pallas import tpu as pltpu
from jax.sharding import PartitionSpec as P

MESH = pl.DeviceIdType.MESH
F32 = jnp.float32
BF16 = jnp.bfloat16
NT = (((1,), (1,)), ((), ()))

DIM = 64
RHS = 32
BLK = 256
AUG = 16
FEAT = DIM + AUG
PAY = FEAT + RHS
SIDE = 16
NEAR = (-1, 4, -3, 5)
FAR = (8, -2, 6, -7)
ROWS = (0,) + NEAR + FAR
F1, F2, M2 = (1, 5), (5, 9), (6, 9)
EXPO = -3.2259641843312467
LIN = 1.3416407864998738


def matern(d2):
    d2 = jnp.maximum(d2, 1e-6)
    r = d2 * lax.rsqrt(d2)
    return ((r * (r + LIN) + 0.6) * jnp.exp2(r * EXPO)).astype(BF16)


def place():
    g, b = lax.axis_index("grp"), lax.axis_index("blk")
    return (b // 4) * 4 + (g // 8) * 2 + (b // 2) % 2, (g % 8) * 2 + b % 2


def device(p, q):
    p, q = lax.rem(p + 32, SIDE), lax.rem(q + 32, SIDE)
    x, y = p // 4, p % 4
    return {"grp": (y // 2) * 8 + q // 2, "blk": x * 4 + (y % 2) * 2 + q % 2}


def slot(k):
    return lax.rem(k + 32, SIDE)


def kernel(pts_hbm, scale_hbm, noise_hbm, res_hbm, dir_hbm, image_out, alpha_out, beta_out,
           pts, scale, noise, res, direc,
           cols, rowpay, rowland, amat, dmat, acc_i, acc_j, back_i, back_j, ks, ks2, ret, stat, stat2, land1, land2,
           in_sem, col_sem, row_sem, pay_sem, fwd_sem, ret_sem, back_sem, s1_sem, s2_sem, st_sem):
    p, q = place()
    turn = 1 - 2 * lax.rem(q, 2)
    barrier = pltpu.get_barrier_semaphore()

    def greet(k, c):
        pl.semaphore_signal(barrier, inc=1, device_id=device(p + k, q), device_id_type=MESH)
        pl.semaphore_signal(barrier, inc=1, device_id=device(p, q + k), device_id_type=MESH)
        return c

    lax.fori_loop(1, SIDE, greet, 0)
    fetch = [pltpu.make_async_copy(a, b, in_sem.at[n]) for n, (a, b) in enumerate(
        ((pts_hbm, pts), (scale_hbm, scale), (dir_hbm, direc), (res_hbm, res), (noise_hbm, noise)))]
    for f in fetch:
        f.start()
    for k in range(SIDE):
        cols[k, PAY:, :] = jnp.zeros((128 - PAY, BLK), BF16)
    acc_i[...] = jnp.zeros_like(acc_i)
    for f in fetch[:3]:
        f.wait()

    at = lax.broadcasted_iota(jnp.int32, (DIM, DIM), 0) == lax.broadcasted_iota(jnp.int32, (DIM, DIM), 1)
    scale_col = jnp.sum(jnp.where(at, scale[...], 0.0), axis=1, keepdims=True)
    scaled = (pts[...] / scale_col).astype(BF16)
    wide = scaled.astype(F32)
    sq = jnp.sum(wide * wide, axis=0, keepdims=True)
    hi = sq.astype(BF16).astype(F32)
    mid = (sq - hi).astype(BF16).astype(F32)
    low = sq - hi - mid
    row = lax.broadcasted_iota(jnp.int32, (AUG, BLK), 0)

    def aug(ones, parts):
        out = jnp.where((row >= ones) & (row < ones + 3), 1.0, 0.0)
        for n, part in enumerate((hi, mid, low)):
            out = jnp.where(row == parts + n, part, out)
        return out.astype(BF16)

    dir_b = direc[...].astype(BF16)
    cols[0, 0:DIM, :] = scaled
    cols[0, DIM:FEAT, :] = aug(0, 3)
    cols[0, FEAT:PAY, :] = dir_b
    rowpay[0:DIM, :] = (wide * -2.0).astype(BF16)
    rowpay[DIM:FEAT, :] = aug(3, 0)
    rowpay[FEAT:PAY, :] = dir_b

    pl.semaphore_wait(barrier, 2 * (SIDE - 1))

    def send_row(k):
        return pltpu.make_async_remote_copy(
            src_ref=rowpay, dst_ref=rowland.at[k], send_sem=pay_sem, recv_sem=row_sem.at[k],
            device_id=device(p - ROWS[k], q), device_id_type=MESH)

    def send_col(k, to=None, sem=None):
        k, to = slot(k), slot(k if to is None else to)
        return pltpu.make_async_remote_copy(
            src_ref=cols.at[k, pl.ds(0, PAY)], dst_ref=cols.at[to, pl.ds(0, PAY)],
            send_sem=pay_sem if sem is None else sem,
            recv_sem=col_sem.at[to], device_id=device(p, q + k - to), device_id_type=MESH)

    def arrived(k):
        send_col(k, k).wait_recv()

    def share_core(k):
        send_col(k, k - turn, fwd_sem).start()

    for k in range(*F1):
        send_row(k).start()
    send_col(0, 2).start()
    send_col(0, -2).start()
    share_core(0)

    def take_row(k, block):
        wide = jnp.concatenate([block[0:FEAT, :], jnp.zeros((128 - FEAT, BLK), BF16)], axis=0)
        amat[k * BLK:(k + 1) * BLK, :] = wide.T
        dmat[:, k * BLK:(k + 1) * BLK] = block[FEAT:PAY, :]

    take_row(0, rowpay)
    for k in (2, -2):
        arrived(k)
        share_core(k)
    send_col(0, 4).start()
    send_col(0, -4).start()
    for k in range(*F1):
        send_row(k).wait_recv()
        take_row(k, rowland.at[k])
    for k in range(*F2):
        send_row(k).start()

    def tile(rows, c):
        a = amat[rows[0] * BLK:rows[1] * BLK, :]
        return matern(jnp.dot(a, cols[slot(c)], preferred_element_type=F32))

    def height(rows):
        return (rows[1] - rows[0]) * BLK

    def give(rows, c, kern, twice=False):
        first = rows[0] + 1 if twice else rows[0]
        skip = (first - rows[0]) * BLK
        k = slot(c)
        part = jnp.dot(dmat[:, first * BLK:rows[1] * BLK], kern[skip:, :], preferred_element_type=F32)
        if rows == F1:
            acc_j[k] = part
        elif isinstance(c, int) and c == 0:
            acc_j[k] += part
        else:
            back_j[k] = (acc_j[k] + part).astype(BF16)
        part = lax.dot_general(cols[k, FEAT:PAY, :], kern, NT, preferred_element_type=F32)
        for n, r in enumerate(range(*rows)):
            acc_i[r] += part[:, n * BLK:(n + 1) * BLK]

    def step(rows, c, old, c_old, src, dst, twice=False):
        new = tile(rows, c)
        give(old, c_old, src[0:height(old), :], twice)
        dst[0:height(rows), :] = new

    def back_row(k):
        return pltpu.make_async_remote_copy(
            src_ref=back_i.at[k - 1], dst_ref=ret.at[k - 1], send_sem=back_sem, recv_sem=ret_sem,
            device_id=device(p + ROWS[k], q), device_id_type=MESH)

    def back_col(k):
        k = slot(k)
        return pltpu.make_async_remote_copy(
            src_ref=back_j.at[k], dst_ref=ret.at[k + 7], send_sem=back_sem, recv_sem=ret_sem,
            device_id=device(p, q + k), device_id_type=MESH)

    def own_tile(n):
        a = amat[0:BLK, :]
        return [matern(jnp.dot(a, cols[4 * n + i], preferred_element_type=F32)) for i in range(4)]

    def own_give(n, src):
        acc_i[0] += sum(lax.dot_general(cols[4 * n + i, FEAT:PAY, :], src[i * BLK:(i + 1) * BLK, :], NT,
                                        preferred_element_type=F32) for i in range(4))

    def own_put(new, dst):
        for i, kern in enumerate(new):
            dst[i * BLK:(i + 1) * BLK, :] = kern

    ks[...] = tile(F1, 0)
    arrived(1)
    arrived(-1)

    def near(n, last):
        k = jnp.where(n < 3, n, 7 - n)

        @pl.when(n == 3)
        def _():
            for k in (4, -4):
                arrived(k)
                share_core(k)
            send_col(4, 6).start()
            send_col(-4, -6).start()
            send_col(4, 8).start()

        @pl.when(n == 4)
        def _():
            arrived(3)
            arrived(-3)

        step(F1, k, F1, last, ks, ks2)
        step(F1, -k, F1, k, ks2, ks)
        return -k

    lax.fori_loop(1, 5, near, jnp.int32(0))

    for k in range(*F2):
        send_row(k).wait_recv()
        take_row(k, rowland.at[k])
    step(F2, 4, F1, -3, ks, ks2)

    def home_near(n, carry):
        m = 4 - n
        step(M2, -m, F2, m, ks2, ks)
        back_col(m).start()
        step(F2, m - 1, M2, -m, ks, ks2)
        back_col(-m).start()
        return carry

    lax.fori_loop(0, 2, home_near, 0)
    for k in (6, -6, 8):
        arrived(k)
        share_core(k)
    step(M2, -2, F2, 2, ks2, ks)
    back_col(2).start()

    for k in (5, -5, 7, -7):
        arrived(k)
    step(F1, 5, M2, -2, ks, ks2)
    back_col(-2).start()

    def far(m, carry):
        step(F1, -m, F1, m, ks2, ks)
        step(F1, m + 1, F1, -m, ks, ks2)
        return carry

    lax.fori_loop(5, 8, far, 0)

    step(F2, 8, F1, 8, ks2, ks)
    for k in range(*F1):
        back_i[k - 1] = acc_i[k].astype(BF16)
        back_row(k).start()
    step(F2, 7, F2, 8, ks, ks2, twice=True)
    back_col(8).start()

    def home(n, carry):
        m = jnp.where(n < 3, 7 - n, 1)
        step(M2, -m, F2, m, ks2, ks)
        back_col(m).start()
        step(F2, jnp.where(n < 2, 6 - n, 3 - n), M2, -m, ks, ks2)
        back_col(-m).start()
        return carry

    lax.fori_loop(0, 4, home, 0)
    new = own_tile(0)
    give(F2, 0, ks2[...], twice=True)
    own_put(new, ks)
    for k in range(*F2):
        back_i[k - 1] = acc_i[k].astype(BF16)
        back_row(k).start()

    for n in range(1, 4):
        src, dst = (ks, ks2) if n % 2 else (ks2, ks)
        new = own_tile(n)
        own_give(n - 1, src)
        own_put(new, dst)
    own_give(3, ks2)

    total = acc_i[0] + acc_j[0]
    for f in fetch[3:]:
        f.wait()
    pltpu.make_async_remote_copy(src_ref=ret, dst_ref=ret, send_sem=back_sem, recv_sem=ret_sem,
                                 device_id=device(p + 1, q), device_id_type=MESH).wait_recv()
    for k in range(23):
        total += ret[k].astype(F32)
    d, r = direc[...], res[...]
    image = total * (5.0 / 3.0) + noise[...] * d
    image_out[...] = image
    lane = lax.broadcasted_iota(jnp.int32, (RHS, 128), 1)
    rhs = lax.broadcasted_iota(jnp.int32, (RHS, 128), 0)

    packed = jnp.zeros((RHS, 128), F32)
    for n, v in enumerate((r * r, d * image, r * image, image * image)):
        packed = jnp.where(lane == rhs + n * RHS, jnp.sum(v, axis=1, keepdims=True), packed)
    stat[...] = jnp.sum(packed, axis=0, keepdims=True)

    def share(src, land, sem, along_p):
        def copy(k):
            to = device(p - k, q) if along_p else device(p, q - k)
            return pltpu.make_async_remote_copy(src_ref=src, dst_ref=land.at[k - 1], send_sem=st_sem,
                                                recv_sem=sem, device_id=to, device_id_type=MESH)

        def start(k, c):
            copy(k).start()
            return c

        lax.fori_loop(1, SIDE, start, 0)
        pltpu.make_async_remote_copy(src_ref=land, dst_ref=land, send_sem=st_sem, recv_sem=sem,
                                     device_id=device(p + 1, q), device_id_type=MESH).wait_recv()
        out = src[...]
        for k in range(SIDE - 1):
            out += land[k]
        return out

    stat2[...] = share(stat, land1, s1_sem, False)
    sums = share(stat2, land2, s2_sem, True)
    rr, curv, rq, qq = (jnp.sum(jnp.where(lane == rhs + n * RHS, sums, 0.0), axis=1, keepdims=True)
                        for n in range(4))
    alpha = rr / curv
    new_rr = rr - alpha * (2.0 * rq - alpha * qq)
    alpha_out[...] = jnp.broadcast_to(alpha, (RHS, BLK))
    beta_out[...] = jnp.broadcast_to(new_rr / rr, (RHS, BLK))

    def sent(ref, sem):
        pltpu.make_async_remote_copy(src_ref=ref, dst_ref=ref, send_sem=sem, recv_sem=ret_sem,
                                     device_id=device(p + 1, q), device_id_type=MESH).wait_send()

    sent(rowland.at[pl.ds(1, 8)], pay_sem)
    for k in range(7):
        sent(rowpay, pay_sem)
    sent(rowland.at[pl.ds(1, 8)], fwd_sem)
    sent(ret, back_sem)
    sent(land1, st_sem)
    sent(land2, st_sem)


def local(points, lengthscale, noise, solution, residual, direction):
    vmem = pl.BlockSpec(memory_space=pltpu.VMEM)
    out = jax.ShapeDtypeStruct((RHS, BLK), F32)
    dma = pltpu.SemaphoreType.DMA
    res_t, dir_t = residual.T, direction.T
    image, alpha, beta = pl.pallas_call(
        kernel,
        out_shape=(out, out, out),
        in_specs=[pl.BlockSpec(memory_space=pltpu.HBM)] * 5,
        out_specs=(vmem,) * 3,
        scratch_shapes=[
            pltpu.VMEM((DIM, BLK), F32),
            pltpu.VMEM((1, DIM), F32),
            pltpu.VMEM((1, BLK), F32),
            pltpu.VMEM((RHS, BLK), F32),
            pltpu.VMEM((RHS, BLK), F32),
            pltpu.VMEM((SIDE, 128, BLK), BF16),
            pltpu.VMEM((PAY, BLK), BF16),
            pltpu.VMEM((9, PAY, BLK), BF16),
            pltpu.VMEM((9 * BLK, 128), BF16),
            pltpu.VMEM((RHS, 9 * BLK), BF16),
            pltpu.VMEM((9, RHS, BLK), F32),
            pltpu.VMEM((SIDE, RHS, BLK), F32),
            pltpu.VMEM((8, RHS, BLK), BF16),
            pltpu.VMEM((SIDE, RHS, BLK), BF16),
            pltpu.VMEM((4 * BLK, BLK), BF16),
            pltpu.VMEM((4 * BLK, BLK), BF16),
            pltpu.VMEM((23, RHS, BLK), BF16),
            pltpu.VMEM((1, 128), F32),
            pltpu.VMEM((1, 128), F32),
            pltpu.VMEM((SIDE - 1, 1, 128), F32),
            pltpu.VMEM((SIDE - 1, 1, 128), F32),
            dma((5,)),
            dma((SIDE,)),
            dma((9,)),
        ] + [dma] * 7,
        compiler_params=pltpu.CompilerParams(
            collective_id=0, has_side_effects=True, vmem_limit_bytes=63 * 2**20),
        name="cg_step",
    )(points.T, lengthscale[None, :], noise[None, :], res_t, dir_t)
    new_sol = solution.T + alpha * dir_t
    new_res = res_t - alpha * image
    new_dir = new_res + beta * dir_t
    return new_sol.T, new_res.T, new_dir.T


def solution(mesh):
    rows = P(("blk", "grp"), None)
    in_specs = (rows, P(), P(("blk", "grp")), rows, rows, rows)
    return jax.shard_map(local, mesh=mesh, in_specs=in_specs, out_specs=(rows,) * 3, check_vma=False)
```

```python
import jax
import jax.numpy as jnp
from jax import lax
from jax.experimental import pallas as pl
from jax.experimental.pallas import tpu as pltpu
from jax.sharding import PartitionSpec as P

MESH = pl.DeviceIdType.MESH
F32 = jnp.float32
BF16 = jnp.bfloat16
NT = (((1,), (1,)), ((), ()))

DIM = 64
RHS = 32
BLK = 256
AUG = 16
FEAT = DIM + AUG
PAY = FEAT + RHS
SIDE = 16
NEAR = (-1, 4, -3, 5)
FAR = (8, -2, 6, -7)
ROWS = (0,) + NEAR + FAR
A1, B1 = (1, 3), (3, 5)
F1, F2, M2 = (1, 5), (5, 9), (6, 9)
FAR_FIRST = (8, 7, 9, 6, 10, 5, 11, 4, 12, 3, 13, 2, 14, 1, 15)
EXPO = -3.2259641843312467
LIN = 1.3416407864998738


def matern(d2):
    d2 = jnp.maximum(d2, 1e-6)
    r = d2 * lax.rsqrt(d2)
    return ((r * (r + LIN) + 0.6) * jnp.exp2(r * EXPO)).astype(BF16)


def place():
    g, b = lax.axis_index("grp"), lax.axis_index("blk")
    return (lax.div(b, 4) * 4 + lax.div(g, 8) * 2 + lax.rem(lax.div(b, 2), 2),
            lax.rem(g, 8) * 2 + lax.rem(b, 2))


def device(p, q):
    p, q = lax.rem(p + 32, SIDE), lax.rem(q + 32, SIDE)
    x, y = lax.div(p, 4), lax.rem(p, 4)
    return {"grp": lax.div(y, 2) * 8 + lax.div(q, 2), "blk": x * 4 + lax.rem(y, 2) * 2 + lax.rem(q, 2)}


def slot(k):
    return lax.rem(k + 32, SIDE)


def kernel(pts_hbm, scale_hbm, noise_hbm, res_hbm, dir_hbm, image_out, alpha_out, beta_out,
           pts, scale, noise, res, direc,
           cols, rowpay, rowland, amat, dmat, acc_i, acc_j, back_i, back_j, ks, ks2, ret, stat, stat2, land1, land2,
           in_sem, col_sem, row_sem, pay_sem, fwd_sem, ret_sem, back_sem, s1_sem, s2_sem, st_sem):
    p, q = place()
    turn = 1 - 2 * lax.rem(q, 2)
    barrier = pltpu.get_barrier_semaphore()

    for k in FAR_FIRST:
        pl.semaphore_signal(barrier, inc=1, device_id=device(p + k, q), device_id_type=MESH)
        pl.semaphore_signal(barrier, inc=1, device_id=device(p, q + k), device_id_type=MESH)
    fetch = [pltpu.make_async_copy(a, b, in_sem.at[n]) for n, (a, b) in enumerate(
        ((pts_hbm, pts), (scale_hbm, scale), (dir_hbm, direc), (res_hbm, res), (noise_hbm, noise)))]
    for f in fetch:
        f.start()
    for k in range(SIDE):
        cols[k, PAY:, :] = jnp.zeros((128 - PAY, BLK), BF16)
    acc_i[...] = jnp.zeros_like(acc_i)
    for f in fetch[:3]:
        f.wait()

    at = lax.broadcasted_iota(jnp.int32, (DIM, DIM), 0) == lax.broadcasted_iota(jnp.int32, (DIM, DIM), 1)
    scale_col = jnp.sum(jnp.where(at, scale[...], 0.0), axis=1, keepdims=True)
    scaled = (pts[...] / scale_col).astype(BF16)
    wide = scaled.astype(F32)
    sq = jnp.sum(wide * wide, axis=0, keepdims=True)
    hi = sq.astype(BF16).astype(F32)
    mid = (sq - hi).astype(BF16).astype(F32)
    low = sq - hi - mid
    row = lax.broadcasted_iota(jnp.int32, (AUG, BLK), 0)

    def aug(ones, parts):
        out = jnp.where((row >= ones) & (row < ones + 3), 1.0, 0.0)
        for n, part in enumerate((hi, mid, low)):
            out = jnp.where(row == parts + n, part, out)
        return out.astype(BF16)

    dir_b = direc[...].astype(BF16)
    cols[0, 0:DIM, :] = scaled
    cols[0, DIM:FEAT, :] = aug(0, 3)
    cols[0, FEAT:PAY, :] = dir_b
    rowpay[0:DIM, :] = (wide * -2.0).astype(BF16)
    rowpay[DIM:FEAT, :] = aug(3, 0)
    rowpay[FEAT:PAY, :] = dir_b

    pl.semaphore_wait(barrier, 2 * (SIDE - 1))

    def send_row(k):
        return pltpu.make_async_remote_copy(
            src_ref=rowpay, dst_ref=rowland.at[k], send_sem=pay_sem, recv_sem=row_sem.at[k],
            device_id=device(p - ROWS[k], q), device_id_type=MESH)

    def send_col(k, to=None, sem=None):
        k, to = slot(k), slot(k if to is None else to)
        return pltpu.make_async_remote_copy(
            src_ref=cols.at[k, pl.ds(0, PAY)], dst_ref=cols.at[to, pl.ds(0, PAY)],
            send_sem=pay_sem if sem is None else sem,
            recv_sem=col_sem.at[to], device_id=device(p, q + k - to), device_id_type=MESH)

    def arrived(k):
        send_col(k, k).wait_recv()

    def share_core(k):
        send_col(k, k - turn, fwd_sem).start()

    for k in range(*F1):
        send_row(k).start()
    send_col(0, 2).start()
    send_col(0, -2).start()
    share_core(0)
    send_col(0, 4).start()
    send_col(0, -4).start()
    for k in range(*F2):
        send_row(k).start()

    def take_row(k, block):
        wide = jnp.concatenate([block[0:FEAT, :], jnp.zeros((128 - FEAT, BLK), BF16)], axis=0)
        amat[k * BLK:(k + 1) * BLK, :] = wide.T
        dmat[:, k * BLK:(k + 1) * BLK] = block[FEAT:PAY, :]

    take_row(0, rowpay)
    for k in (2, -2):
        arrived(k)
        share_core(k)
    for k in range(*A1):
        send_row(k).wait_recv()
        take_row(k, rowland.at[k])

    def tile(rows, c):
        a = amat[rows[0] * BLK:rows[1] * BLK, :]
        return matern(jnp.dot(a, cols[slot(c)], preferred_element_type=F32))

    def height(rows):
        return (rows[1] - rows[0]) * BLK

    def give(rows, c, kern, twice=False):
        first = rows[0] + 1 if twice else rows[0]
        skip = (first - rows[0]) * BLK
        k = slot(c)
        part = jnp.dot(dmat[:, first * BLK:rows[1] * BLK], kern[skip:, :], preferred_element_type=F32)
        if rows in (A1, F1):
            acc_j[k] = part
        elif rows == B1:
            acc_j[k] += part
        elif isinstance(c, int) and c == 0:
            acc_j[k] += part
        else:
            back_j[k] = (acc_j[k] + part).astype(BF16)
        part = lax.dot_general(cols[k, FEAT:PAY, :], kern, NT, preferred_element_type=F32)
        for n, r in enumerate(range(*rows)):
            acc_i[r] += part[:, n * BLK:(n + 1) * BLK]

    def step(rows, c, old, c_old, src, dst, twice=False):
        new = tile(rows, c)
        give(old, c_old, src[0:height(old), :], twice)
        dst[0:height(rows), :] = new

    def back_row(k):
        return pltpu.make_async_remote_copy(
            src_ref=back_i.at[k - 1], dst_ref=ret.at[k - 1], send_sem=back_sem, recv_sem=ret_sem,
            device_id=device(p + ROWS[k], q), device_id_type=MESH)

    def back_col(k):
        k = slot(k)
        return pltpu.make_async_remote_copy(
            src_ref=back_j.at[k], dst_ref=ret.at[k + 7], send_sem=back_sem, recv_sem=ret_sem,
            device_id=device(p, q + k), device_id_type=MESH)

    def own_tile(n):
        a = amat[0:BLK, :]
        return [matern(jnp.dot(a, cols[4 * n + i], preferred_element_type=F32)) for i in range(4)]

    def own_give(n, src):
        acc_i[0] += sum(lax.dot_general(cols[4 * n + i, FEAT:PAY, :], src[i * BLK:(i + 1) * BLK, :], NT,
                                        preferred_element_type=F32) for i in range(4))

    def own_put(new, dst):
        for i, kern in enumerate(new):
            dst[i * BLK:(i + 1) * BLK, :] = kern

    ks2[0:height(A1), :] = tile(A1, 0)
    step(A1, 2, A1, 0, ks2, ks)
    step(A1, -2, A1, 2, ks, ks2)
    arrived(1)
    arrived(-1)
    step(A1, 1, A1, -2, ks2, ks)
    step(A1, -1, A1, 1, ks, ks2)
    for k in (4, -4):
        arrived(k)
        share_core(k)
    send_col(4, 6).start()
    send_col(-4, -6).start()
    send_col(4, 8).start()
    for k in range(*B1):
        send_row(k).wait_recv()
        take_row(k, rowland.at[k])
    step(B1, 0, A1, -1, ks2, ks)
    step(B1, 2, B1, 0, ks, ks2)
    step(B1, -2, B1, 2, ks2, ks)
    step(B1, 1, B1, -2, ks, ks2)
    step(B1, -1, B1, 1, ks2, ks)
    step(F1, 4, B1, -1, ks, ks2)
    step(F1, -4, F1, 4, ks2, ks)
    arrived(3)
    arrived(-3)
    step(F1, 3, F1, -4, ks, ks2)
    step(F1, -3, F1, 3, ks2, ks)

    for k in range(*F2):
        send_row(k).wait_recv()
        take_row(k, rowland.at[k])
    step(F2, 4, F1, -3, ks, ks2)

    def home_near(n, carry):
        m = 4 - n
        step(M2, -m, F2, m, ks2, ks)
        back_col(m).start()
        step(F2, m - 1, M2, -m, ks, ks2)
        back_col(-m).start()
        return carry

    lax.fori_loop(0, 2, home_near, 0)
    for k in (6, -6, 8):
        arrived(k)
        share_core(k)
    step(M2, -2, F2, 2, ks2, ks)
    back_col(2).start()

    for k in (5, -5, 7, -7):
        arrived(k)
    step(F1, 5, M2, -2, ks, ks2)
    back_col(-2).start()

    def far(m, carry):
        step(F1, -m, F1, m, ks2, ks)
        step(F1, m + 1, F1, -m, ks, ks2)
        return carry

    lax.fori_loop(5, 8, far, 0)

    step(F2, 8, F1, 8, ks2, ks)
    for k in range(*F1):
        back_i[k - 1] = acc_i[k].astype(BF16)
        back_row(k).start()
    step(F2, 7, F2, 8, ks, ks2, twice=True)
    back_col(8).start()

    def home(n, carry):
        m = jnp.where(n < 3, 7 - n, 1)
        step(M2, -m, F2, m, ks2, ks)
        back_col(m).start()
        step(F2, jnp.where(n < 2, 6 - n, 3 - n), M2, -m, ks, ks2)
        back_col(-m).start()
        return carry

    lax.fori_loop(0, 4, home, 0)
    new = own_tile(0)
    give(F2, 0, ks2[...], twice=True)
    own_put(new, ks)
    for k in range(*F2):
        back_i[k - 1] = acc_i[k].astype(BF16)
        back_row(k).start()

    for n in range(1, 4):
        src, dst = (ks, ks2) if n % 2 else (ks2, ks)
        new = own_tile(n)
        own_give(n - 1, src)
        own_put(new, dst)
    own_give(3, ks2)

    total = acc_i[0] + acc_j[0]
    for f in fetch[3:]:
        f.wait()
    pltpu.make_async_remote_copy(src_ref=ret, dst_ref=ret, send_sem=back_sem, recv_sem=ret_sem,
                                 device_id=device(p + 1, q), device_id_type=MESH).wait_recv()
    for k in range(23):
        total += ret[k].astype(F32)
    d, r = direc[...], res[...]
    image = total * (5.0 / 3.0) + noise[...] * d
    image_out[...] = image
    lane = lax.broadcasted_iota(jnp.int32, (RHS, 128), 1)
    rhs = lax.broadcasted_iota(jnp.int32, (RHS, 128), 0)

    packed = jnp.zeros((RHS, 128), F32)
    for n, v in enumerate((r * r, d * image, r * image, image * image)):
        packed = jnp.where(lane == rhs + n * RHS, jnp.sum(v, axis=1, keepdims=True), packed)
    stat[...] = jnp.sum(packed, axis=0, keepdims=True)

    def share(src, land, sem, along_p):
        def copy(k):
            to = device(p - k, q) if along_p else device(p, q - k)
            return pltpu.make_async_remote_copy(src_ref=src, dst_ref=land.at[k - 1], send_sem=st_sem,
                                                recv_sem=sem, device_id=to, device_id_type=MESH)

        for k in FAR_FIRST:
            copy(k).start()
        pltpu.make_async_remote_copy(src_ref=land, dst_ref=land, send_sem=st_sem, recv_sem=sem,
                                     device_id=device(p + 1, q), device_id_type=MESH).wait_recv()
        out = src[...]
        for k in range(SIDE - 1):
            out += land[k]
        return out

    stat2[...] = share(stat, land1, s1_sem, False)
    sums = share(stat2, land2, s2_sem, True)
    rr, curv, rq, qq = (jnp.sum(jnp.where(lane == rhs + n * RHS, sums, 0.0), axis=1, keepdims=True)
                        for n in range(4))
    alpha = rr / curv
    new_rr = rr - alpha * (2.0 * rq - alpha * qq)
    alpha_out[...] = jnp.broadcast_to(alpha, (RHS, BLK))
    beta_out[...] = jnp.broadcast_to(new_rr / rr, (RHS, BLK))

    def sent(ref, sem):
        pltpu.make_async_remote_copy(src_ref=ref, dst_ref=ref, send_sem=sem, recv_sem=ret_sem,
                                     device_id=device(p + 1, q), device_id_type=MESH).wait_send()

    sent(rowland.at[pl.ds(1, 8)], pay_sem)
    for k in range(7):
        sent(rowpay, pay_sem)
    sent(rowland.at[pl.ds(1, 8)], fwd_sem)
    sent(ret, back_sem)
    sent(land1, st_sem)
    sent(land2, st_sem)


def local(points, lengthscale, noise, solution, residual, direction):
    vmem = pl.BlockSpec(memory_space=pltpu.VMEM)
    out = jax.ShapeDtypeStruct((RHS, BLK), F32)
    dma = pltpu.SemaphoreType.DMA
    res_t, dir_t = residual.T, direction.T
    image, alpha, beta = pl.pallas_call(
        kernel,
        out_shape=(out, out, out),
        in_specs=[pl.BlockSpec(memory_space=pltpu.HBM)] * 5,
        out_specs=(vmem,) * 3,
        scratch_shapes=[
            pltpu.VMEM((DIM, BLK), F32),
            pltpu.VMEM((1, DIM), F32),
            pltpu.VMEM((1, BLK), F32),
            pltpu.VMEM((RHS, BLK), F32),
            pltpu.VMEM((RHS, BLK), F32),
            pltpu.VMEM((SIDE, 128, BLK), BF16),
            pltpu.VMEM((PAY, BLK), BF16),
            pltpu.VMEM((9, PAY, BLK), BF16),
            pltpu.VMEM((9 * BLK, 128), BF16),
            pltpu.VMEM((RHS, 9 * BLK), BF16),
            pltpu.VMEM((9, RHS, BLK), F32),
            pltpu.VMEM((SIDE, RHS, BLK), F32),
            pltpu.VMEM((8, RHS, BLK), BF16),
            pltpu.VMEM((SIDE, RHS, BLK), BF16),
            pltpu.VMEM((4 * BLK, BLK), BF16),
            pltpu.VMEM((4 * BLK, BLK), BF16),
            pltpu.VMEM((23, RHS, BLK), BF16),
            pltpu.VMEM((1, 128), F32),
            pltpu.VMEM((1, 128), F32),
            pltpu.VMEM((SIDE - 1, 1, 128), F32),
            pltpu.VMEM((SIDE - 1, 1, 128), F32),
            dma((5,)),
            dma((SIDE,)),
            dma((9,)),
        ] + [dma] * 7,
        compiler_params=pltpu.CompilerParams(
            collective_id=0, has_side_effects=True, vmem_limit_bytes=63 * 2**20),
        name="cg_step",
    )(points.T, lengthscale[None, :], noise[None, :], res_t, dir_t)
    new_sol = solution.T + alpha * dir_t
    new_res = res_t - alpha * image
    new_dir = new_res + beta * dir_t
    return new_sol.T, new_res.T, new_dir.T


def solution(mesh):
    rows = P(("blk", "grp"), None)
    in_specs = (rows, P(), P(("blk", "grp")), rows, rows, rows)
    return jax.shard_map(local, mesh=mesh, in_specs=in_specs, out_specs=(rows,) * 3, check_vma=False)
```

```python
import jax
import jax.numpy as jnp
from jax import lax
from jax.experimental import pallas as pl
from jax.experimental.pallas import tpu as pltpu
from jax.sharding import PartitionSpec as P

MESH = pl.DeviceIdType.MESH
F32 = jnp.float32
BF16 = jnp.bfloat16
NT = (((1,), (1,)), ((), ()))

DIM = 64
RHS = 32
BLK = 256
AUG = 16
FEAT = DIM + AUG
PAY = FEAT + RHS
SIDE = 16
NEAR = (-1, 4, -3, 5)
FAR = (8, -2, 6, -7)
ROWS = (0,) + NEAR + FAR
A1, B1 = (1, 3), (3, 5)
F1, F2, M2 = (1, 5), (5, 9), (6, 9)
FAR_FIRST = (8, 7, 9, 6, 10, 5, 11, 4, 12, 3, 13, 2, 14, 1, 15)
EXPO = -3.2259641843312467
LIN = 1.3416407864998738


def matern(d2):
    d2 = jnp.maximum(d2, 1e-6)
    r = d2 * lax.rsqrt(d2)
    return ((r * (r + LIN) + 0.6) * jnp.exp2(r * EXPO)).astype(BF16)


def place():
    g, b = lax.axis_index("grp"), lax.axis_index("blk")
    return (lax.div(b, 4) * 4 + lax.div(g, 8) * 2 + lax.rem(lax.div(b, 2), 2),
            lax.rem(g, 8) * 2 + lax.rem(b, 2))


def device(p, q):
    p, q = lax.rem(p + 32, SIDE), lax.rem(q + 32, SIDE)
    x, y = lax.div(p, 4), lax.rem(p, 4)
    return {"grp": lax.div(y, 2) * 8 + lax.div(q, 2), "blk": x * 4 + lax.rem(y, 2) * 2 + lax.rem(q, 2)}


def slot(k):
    return lax.rem(k + 32, SIDE)


def kernel(pts_hbm, scale_hbm, noise_hbm, res_hbm, dir_hbm, image_out, alpha_out, beta_out,
           pts, scale, noise, res, direc,
           cols, rowpay, rowland, amat, dmat, acc_i, acc_j, back_i, back_j, ks, ks2, ret, stat, stat2, land1, land2,
           in_sem, col_sem, row_sem, pay_sem, fwd_sem, ret_sem, back_sem, s1_sem, s2_sem, st_sem):
    p, q = place()
    turn = 1 - 2 * lax.rem(q, 2)
    fetch = [pltpu.make_async_copy(a, b, in_sem.at[n]) for n, (a, b) in enumerate(
        ((pts_hbm, pts), (scale_hbm, scale), (dir_hbm, direc), (res_hbm, res), (noise_hbm, noise)))]
    for f in fetch:
        f.start()
    barrier = pltpu.get_barrier_semaphore()

    for k in FAR_FIRST:
        pl.semaphore_signal(barrier, inc=1, device_id=device(p + k, q), device_id_type=MESH)
        pl.semaphore_signal(barrier, inc=1, device_id=device(p, q + k), device_id_type=MESH)
    for k in range(SIDE):
        cols[k, PAY:, :] = jnp.zeros((128 - PAY, BLK), BF16)
    for f in fetch[:3]:
        f.wait()

    at = lax.broadcasted_iota(jnp.int32, (DIM, DIM), 0) == lax.broadcasted_iota(jnp.int32, (DIM, DIM), 1)
    scale_col = jnp.sum(jnp.where(at, scale[...], 0.0), axis=1, keepdims=True)
    scaled = (pts[...] / scale_col).astype(BF16)
    wide = scaled.astype(F32)
    sq = jnp.sum(wide * wide, axis=0, keepdims=True)
    hi = sq.astype(BF16).astype(F32)
    mid = (sq - hi).astype(BF16).astype(F32)
    low = sq - hi - mid
    row = lax.broadcasted_iota(jnp.int32, (AUG, BLK), 0)

    def aug(ones, parts):
        out = jnp.where((row >= ones) & (row < ones + 3), 1.0, 0.0)
        for n, part in enumerate((hi, mid, low)):
            out = jnp.where(row == parts + n, part, out)
        return out.astype(BF16)

    dir_b = direc[...].astype(BF16)
    cols[0, 0:DIM, :] = scaled
    cols[0, DIM:FEAT, :] = aug(0, 3)
    cols[0, FEAT:PAY, :] = dir_b
    rowpay[0:DIM, :] = (wide * -2.0).astype(BF16)
    rowpay[DIM:FEAT, :] = aug(3, 0)
    rowpay[FEAT:PAY, :] = dir_b

    pl.semaphore_wait(barrier, 2 * (SIDE - 1))

    def send_row(k):
        return pltpu.make_async_remote_copy(
            src_ref=rowpay, dst_ref=rowland.at[k], send_sem=pay_sem, recv_sem=row_sem.at[k],
            device_id=device(p - ROWS[k], q), device_id_type=MESH)

    def send_col(k, to=None, sem=None):
        k, to = slot(k), slot(k if to is None else to)
        return pltpu.make_async_remote_copy(
            src_ref=cols.at[k, pl.ds(0, PAY)], dst_ref=cols.at[to, pl.ds(0, PAY)],
            send_sem=pay_sem if sem is None else sem,
            recv_sem=col_sem.at[to], device_id=device(p, q + k - to), device_id_type=MESH)

    def arrived(k):
        send_col(k, k).wait_recv()

    def share_core(k):
        send_col(k, k - turn, fwd_sem).start()

    for k in range(*F1):
        send_row(k).start()
    send_col(0, 2).start()
    send_col(0, -2).start()
    share_core(0)
    send_col(0, 4).start()
    send_col(0, -4).start()
    for k in range(*F2):
        send_row(k).start()

    def take_row(k, block):
        wide = jnp.concatenate([block[0:FEAT, :], jnp.zeros((128 - FEAT, BLK), BF16)], axis=0)
        amat[k * BLK:(k + 1) * BLK, :] = wide.T
        dmat[:, k * BLK:(k + 1) * BLK] = block[FEAT:PAY, :]

    acc_i[...] = jnp.zeros_like(acc_i)
    take_row(0, rowpay)
    for k in (2, -2):
        arrived(k)
        share_core(k)
    for k in range(*A1):
        send_row(k).wait_recv()
        take_row(k, rowland.at[k])

    def tile(rows, c):
        a = amat[rows[0] * BLK:rows[1] * BLK, :]
        return matern(jnp.dot(a, cols[slot(c)], preferred_element_type=F32))

    def height(rows):
        return (rows[1] - rows[0]) * BLK

    far_cols = [False]

    def give(rows, c, kern, twice=False):
        first = rows[0] + 1 if twice else rows[0]
        skip = (first - rows[0]) * BLK
        k = slot(c)
        part = jnp.dot(dmat[:, first * BLK:rows[1] * BLK], kern[skip:, :], preferred_element_type=F32)
        near_rows = rows[1] <= F1[1]
        if rows == B1 or (isinstance(c, int) and c == 0 and not near_rows):
            acc_j[k] += part
        elif near_rows != far_cols[0]:
            acc_j[k] = part
        else:
            back_j[k] = (acc_j[k] + part).astype(BF16)
        part = lax.dot_general(cols[k, FEAT:PAY, :], kern, NT, preferred_element_type=F32)
        for n, r in enumerate(range(*rows)):
            acc_i[r] += part[:, n * BLK:(n + 1) * BLK]

    def step(rows, c, old, c_old, src, dst, twice=False):
        new = tile(rows, c)
        give(old, c_old, src[0:height(old), :], twice)
        dst[0:height(rows), :] = new

    def back_row(k):
        return pltpu.make_async_remote_copy(
            src_ref=back_i.at[k - 1], dst_ref=ret.at[k - 1], send_sem=back_sem, recv_sem=ret_sem,
            device_id=device(p + ROWS[k], q), device_id_type=MESH)

    def back_col(k):
        k = slot(k)
        return pltpu.make_async_remote_copy(
            src_ref=back_j.at[k], dst_ref=ret.at[k + 7], send_sem=back_sem, recv_sem=ret_sem,
            device_id=device(p, q + k), device_id_type=MESH)

    def own_tile(n):
        a = amat[0:BLK, :]
        return [matern(jnp.dot(a, cols[4 * n + i], preferred_element_type=F32)) for i in range(4)]

    def own_give(n, src):
        acc_i[0] += sum(lax.dot_general(cols[4 * n + i, FEAT:PAY, :], src[i * BLK:(i + 1) * BLK, :], NT,
                                        preferred_element_type=F32) for i in range(4))

    def own_put(new, dst):
        for i, kern in enumerate(new):
            dst[i * BLK:(i + 1) * BLK, :] = kern

    ks2[0:height(A1), :] = tile(A1, 0)
    step(A1, 2, A1, 0, ks2, ks)
    step(A1, -2, A1, 2, ks, ks2)
    arrived(1)
    arrived(-1)
    step(A1, 1, A1, -2, ks2, ks)
    step(A1, -1, A1, 1, ks, ks2)
    for k in (4, -4):
        arrived(k)
    send_col(4, 6).start()
    send_col(-4, -6).start()
    send_col(4, 8).start()
    for k in (4, -4):
        share_core(k)
    for k in range(*B1):
        send_row(k).wait_recv()
        take_row(k, rowland.at[k])
    step(B1, 0, A1, -1, ks2, ks)
    step(B1, 2, B1, 0, ks, ks2)
    step(B1, -2, B1, 2, ks2, ks)
    step(B1, 1, B1, -2, ks, ks2)
    step(B1, -1, B1, 1, ks2, ks)
    step(F1, 4, B1, -1, ks, ks2)
    step(F1, -4, F1, 4, ks2, ks)
    arrived(3)
    arrived(-3)
    step(F1, 3, F1, -4, ks, ks2)
    step(F1, -3, F1, 3, ks2, ks)

    for k in range(*F2):
        send_row(k).wait_recv()
        take_row(k, rowland.at[k])
    step(F2, 4, F1, -3, ks, ks2)

    def home_near(n, carry):
        m = 4 - n

        @pl.when(n == 2)
        def _():
            for k in (6, -6, 8):
                arrived(k)
                share_core(k)

        step(M2, -m, F2, m, ks2, ks)
        back_col(m).start()
        step(F2, m - 1, M2, -m, ks, ks2)
        back_col(-m).start()
        return carry

    lax.fori_loop(0, 4, home_near, 0)

    for k in (5, -5, 7, -7):
        arrived(k)
    step(F2, 8, F2, 0, ks2, ks, twice=True)
    far_cols[0] = True
    step(F2, 7, F2, 8, ks, ks2, twice=True)

    def far(n, carry):
        m = 7 - n
        step(M2, -m, F2, m, ks2, ks)
        step(F2, m - 1, M2, -m, ks, ks2)
        return carry

    lax.fori_loop(0, 2, far, 0)
    step(M2, -5, F2, 5, ks2, ks)

    step(F1, 8, M2, -5, ks, ks2)
    for k in range(*F2):
        back_i[k - 1] = acc_i[k].astype(BF16)
        back_row(k).start()
    step(F1, 7, F1, 8, ks2, ks)
    back_col(8).start()

    def home(n, carry):
        m = 7 - n
        step(F1, -m, F1, m, ks, ks2)
        back_col(m).start()
        step(F1, m - 1, F1, -m, ks2, ks)
        back_col(-m).start()
        return carry

    lax.fori_loop(0, 2, home, 0)
    step(F1, -5, F1, 5, ks, ks2)
    back_col(5).start()
    new = own_tile(0)
    give(F1, -5, ks2[...])
    back_col(-5).start()
    own_put(new, ks)
    for k in range(*F1):
        back_i[k - 1] = acc_i[k].astype(BF16)
        back_row(k).start()

    for n in range(1, 4):
        src, dst = (ks, ks2) if n % 2 else (ks2, ks)
        new = own_tile(n)
        own_give(n - 1, src)
        own_put(new, dst)
    own_give(3, ks2)

    total = acc_i[0] + acc_j[0]
    for f in fetch[3:]:
        f.wait()
    d, r = direc[...], res[...]
    total = total * (5.0 / 3.0) + noise[...] * d
    rr = jnp.sum(r * r, axis=1, keepdims=True)
    pltpu.make_async_remote_copy(src_ref=ret, dst_ref=ret, send_sem=back_sem, recv_sem=ret_sem,
                                 device_id=device(p + 1, q), device_id_type=MESH).wait_recv()
    parts = [ret[k].astype(F32) for k in range(23)]
    while len(parts) > 1:
        parts = [sum(parts[n:n + 2]) for n in range(0, len(parts), 2)]
    image = total + parts[0] * (5.0 / 3.0)
    image_out[...] = image
    lane = lax.broadcasted_iota(jnp.int32, (RHS, 128), 1)
    rhs = lax.broadcasted_iota(jnp.int32, (RHS, 128), 0)

    packed = jnp.zeros((RHS, 128), F32)
    for n, v in enumerate((rr, *(jnp.sum(v * image, axis=1, keepdims=True) for v in (d, r, image)))):
        packed = jnp.where(lane == rhs + n * RHS, v, packed)
    stat[...] = jnp.sum(packed, axis=0, keepdims=True)

    def sent(ref, sem):
        pltpu.make_async_remote_copy(src_ref=ref, dst_ref=ref, send_sem=sem, recv_sem=ret_sem,
                                     device_id=device(p + 1, q), device_id_type=MESH).wait_send()

    def share(src, land, sem, along_p):
        def copy(k):
            to = device(p - k, q) if along_p else device(p, q - k)
            return pltpu.make_async_remote_copy(src_ref=src, dst_ref=land.at[k - 1], send_sem=st_sem,
                                                recv_sem=sem, device_id=to, device_id_type=MESH)

        for k in FAR_FIRST:
            copy(k).start()
        if not along_p:
            sent(rowland.at[pl.ds(1, 8)], pay_sem)
            for k in range(7):
                sent(rowpay, pay_sem)
            sent(rowland.at[pl.ds(1, 8)], fwd_sem)
            sent(ret, back_sem)
        pltpu.make_async_remote_copy(src_ref=land, dst_ref=land, send_sem=st_sem, recv_sem=sem,
                                     device_id=device(p + 1, q), device_id_type=MESH).wait_recv()
        out = src[...]
        for k in range(SIDE - 1):
            out += land[k]
        return out

    stat2[...] = share(stat, land1, s1_sem, False)
    sums = share(stat2, land2, s2_sem, True)
    rr, curv, rq, qq = (jnp.sum(jnp.where(lane == rhs + n * RHS, sums, 0.0), axis=1, keepdims=True)
                        for n in range(4))
    alpha = rr / curv
    new_rr = rr - alpha * (2.0 * rq - alpha * qq)
    alpha_out[...] = jnp.broadcast_to(alpha, (RHS, BLK))
    beta_out[...] = jnp.broadcast_to(new_rr / rr, (RHS, BLK))

    sent(land1, st_sem)
    sent(land2, st_sem)


def local(points, lengthscale, noise, solution, residual, direction):
    vmem = pl.BlockSpec(memory_space=pltpu.VMEM)
    out = jax.ShapeDtypeStruct((RHS, BLK), F32)
    dma = pltpu.SemaphoreType.DMA
    res_t, dir_t = residual.T, direction.T
    image, alpha, beta = pl.pallas_call(
        kernel,
        out_shape=(out, out, out),
        in_specs=[pl.BlockSpec(memory_space=pltpu.HBM)] * 5,
        out_specs=(vmem,) * 3,
        scratch_shapes=[
            pltpu.VMEM((DIM, BLK), F32),
            pltpu.VMEM((1, DIM), F32),
            pltpu.VMEM((1, BLK), F32),
            pltpu.VMEM((RHS, BLK), F32),
            pltpu.VMEM((RHS, BLK), F32),
            pltpu.VMEM((SIDE, 128, BLK), BF16),
            pltpu.VMEM((PAY, BLK), BF16),
            pltpu.VMEM((9, PAY, BLK), BF16),
            pltpu.VMEM((9 * BLK, 128), BF16),
            pltpu.VMEM((RHS, 9 * BLK), BF16),
            pltpu.VMEM((9, RHS, BLK), F32),
            pltpu.VMEM((SIDE, RHS, BLK), F32),
            pltpu.VMEM((8, RHS, BLK), BF16),
            pltpu.VMEM((SIDE, RHS, BLK), BF16),
            pltpu.VMEM((4 * BLK, BLK), BF16),
            pltpu.VMEM((4 * BLK, BLK), BF16),
            pltpu.VMEM((23, RHS, BLK), BF16),
            pltpu.VMEM((1, 128), F32),
            pltpu.VMEM((1, 128), F32),
            pltpu.VMEM((SIDE - 1, 1, 128), F32),
            pltpu.VMEM((SIDE - 1, 1, 128), F32),
            dma((5,)),
            dma((SIDE,)),
            dma((9,)),
        ] + [dma] * 7,
        compiler_params=pltpu.CompilerParams(
            collective_id=0, has_side_effects=True, vmem_limit_bytes=63 * 2**20),
        name="cg_step",
    )(points.T, lengthscale[None, :], noise[None, :], res_t, dir_t)
    new_sol = solution.T + alpha * dir_t
    new_res = res_t - alpha * image
    new_dir = new_res + beta * dir_t
    return new_sol.T, new_res.T, new_dir.T


def solution(mesh):
    rows = P(("blk", "grp"), None)
    in_specs = (rows, P(), P(("blk", "grp")), rows, rows, rows)
    return jax.shard_map(local, mesh=mesh, in_specs=in_specs, out_specs=(rows,) * 3, check_vma=False)
```
